1024 devices in a mesh: blk: 256 (over y, z, x_lo), rep: 4 (over x_hi, core).
Axes of the slice: x: 4 (x_hi: 2, x_lo: 2; x = x_hi * 2 + x_lo), y: 4, z: 32, core: 2. Of those that a mesh axis runs over, the one named last changes fastest.
Arguments:
- features: bfloat16 [131072, 256], P('blk'), may hold values from -6 to 6
- tile_vals: bfloat16 [1024, 64, 128, 128], P('blk', None, 'rep'), may hold values from -0.0625 to 0.0625
- tile_cols: int32 [1024, 64], P('blk'), may hold values from 0 to 1023, as said below
- tile_count: int32 [1024], P('blk'), may hold values from 16 to 64, as said below
- weight: bfloat16 [256, 256], replicated, may hold values from -0.375 to 0.375
- bias: float32 [256], replicated, may hold values from -3 to 3
- cotangent: bfloat16 [131072, 256], P(('blk', 'rep')), may hold values from -6 to 6
Outputs:
- activated: bfloat16 [131072, 256], P(('blk', 'rep'))
- weight_grad: float32 [256, 256], replicated
- bias_grad: float32 [256], replicated
The draws below stay inside these ranges and needn't reach their ends.
Inputs may be any that keep to these rules, and one draw needn't show every extreme that they name: Entries of one row of tile_cols are distinct; slot 0 of row block i holds i; for every column block j of row block i, j // 4 and i // 4 differ by at most 16, counted cyclically modulo 1024 // 4, and every row block has a column block at that distance on each side. `tile_count`: some row block uses all 64 slots.
All inputs are finite; a program needn't handle non-finite values.
Results may differ from the reference program's by a relative error of at most 0.007.
Values may be sent and summed in bfloat16 or wider, within the bound.
A program may use at most 32 MiB of HBM per device.

```python
import jax
import jax.numpy as jnp
from jax import lax

F = 256
TILE = 128
BLK_DEV = 4
REACH = 16
TILE_MOST = 64
BLOCKS = 1024
NODES = 131072
N_BLK = 256


def draw_tile_cols(key, part):
    key = jax.random.fold_in(key, 11)
    span = (2 * REACH + 1) * BLK_DEV
    row_ids = jnp.arange(BLOCKS, dtype=jnp.int32)
    places = jnp.arange(span, dtype=jnp.int32)
    scores = jax.random.randint(key, (BLOCKS, span), 0, 1 << 20) * span + places[None, :]
    own = (REACH * BLK_DEV + row_ids % BLK_DEV)[:, None]
    scores = jnp.where(places[None, :] == span - 1, -1, scores)
    scores = jnp.where(places[None, :] == 0, -2, scores)
    scores = jnp.where(places[None, :] == own, -3, scores)
    order = jnp.argsort(scores, axis=1, stable=True).astype(jnp.int32)[:, :TILE_MOST]
    group = (row_ids // BLK_DEV)[:, None] - REACH + order // BLK_DEV
    group = jnp.mod(group, N_BLK)
    return (group * BLK_DEV + order % BLK_DEV).astype(jnp.int32)


def draw_tile_count(key, part):
    key = jax.random.fold_in(key, 23)
    first, second = jax.random.split(key)
    counts = jax.random.randint(first, (BLOCKS,), TILE_MOST // 4, TILE_MOST + 1)
    fullest = jax.random.randint(second, (), 0, BLOCKS)
    counts = jnp.where(jnp.arange(BLOCKS, dtype=jnp.int32) == fullest, TILE_MOST, counts)
    return counts.astype(jnp.int32)


def level_of(rng, dims, cuts, low, high):
    factor_of = 1.0
    for dim, shards_of in cuts:
        draws = jax.random.uniform(jax.random.fold_in(jax.random.fold_in(rng, 6), dim), (shards_of,), jnp.float32, low / len(cuts), high / len(cuts))
        factor_of = factor_of * jnp.repeat(jnp.exp(draws), dims[dim] // shards_of).reshape((-1,) + (1,) * (len(dims) - 1 - dim))
    return factor_of


def normal_values(key, shape, scale, limit, cuts=(), held_as=jnp.bfloat16):
    array = scale * jax.random.normal(key, shape, jnp.float32)
    if cuts:
        array = array * level_of(key, shape, cuts, -0.22, 0.18)
    return jnp.clip(array, -limit, limit).astype(held_as)


def setup_inputs(seed: int = 0) -> dict:
    key_list = jax.random.split(jax.random.key(seed), 8)
    features = normal_values(key_list[0], (NODES, F), 1.0, 6.0, ((0, 256),))
    tile_vals = normal_values(key_list[1], (BLOCKS, TILE_MOST, TILE, TILE), (TILE * TILE_MOST) ** -0.5, 0.0625, ((0, 256), (2, 4)))
    tile_cols = draw_tile_cols(jax.random.fold_in(key_list[7], 71), 0)
    tile_count = draw_tile_count(jax.random.fold_in(key_list[7], 71), 0)
    weight = normal_values(key_list[4], (F, F), F ** -0.5, 0.375)
    bias = normal_values(key_list[5], (F,), 0.5, 3.0, (), jnp.float32)
    cotangent = normal_values(key_list[6], (NODES, F), 1.0, 6.0, ((0, 1024),))
    return dict(features=features, tile_vals=tile_vals, tile_cols=tile_cols, tile_count=tile_count, weight=weight, bias=bias, cotangent=cotangent)


def reference(features, tile_vals, tile_cols, tile_count, weight, bias, cotangent):
    n_blocks = tile_cols.shape[0]
    slots = tile_cols.shape[1]
    tile = tile_vals.shape[2]
    width = features.shape[1]
    blocks = features.reshape(n_blocks, tile, width)

    def one_row(packed):
        vals, cols, count = packed
        valid = (jnp.arange(slots, dtype=jnp.int32) < count).astype(jnp.float32)
        picked = blocks[cols].astype(jnp.float32)
        scaled = vals.astype(jnp.float32) * valid[:, None, None]
        return jnp.einsum('sca,scf->af', scaled, picked)
    rows = lax.map(one_row, (tile_vals, tile_cols, tile_count))
    aggregated = rows.reshape(n_blocks * tile, width).astype(jnp.bfloat16)
    pre = jnp.dot(aggregated, weight, preferred_element_type=jnp.float32) + bias
    activated = jax.nn.silu(pre).astype(jnp.bfloat16)
    sig = jax.nn.sigmoid(pre)
    grad_pre = (cotangent.astype(jnp.float32) * sig * (1.0 + pre * (1.0 - sig))).astype(jnp.bfloat16)
    scale = 1.0 / jnp.sqrt(jnp.float32(n_blocks * tile))
    weight_grad = lax.dot_general(aggregated, grad_pre, (((0,), (0,)), ((), ())), preferred_element_type=jnp.float32) * scale
    bias_grad = lax.optimization_barrier(jnp.sum(grad_pre.astype(jnp.float32), axis=0)) * scale
    return (activated, weight_grad, bias_grad)
```

```python
import math

import jax
import jax.numpy as jnp
from jax import lax
from jax.experimental import pallas as pl
from jax.experimental.pallas import tpu as pltpu
from jax.sharding import PartitionSpec as P

STEPS = 8
ZL = 8
ZH = 4
Y = 4
X = 4
STOP = 99


def dev(b, r):
    return {"blk": b, "rep": r}


def rcopy(src, dst, ssem, rsem, to):
    return pltpu.make_async_remote_copy(
        src_ref=src,
        dst_ref=dst,
        send_sem=ssem,
        recv_sem=rsem,
        device_id=to,
        device_id_type=pl.DeviceIdType.MESH,
    )


def kernel(
    cols,
    cnt,
    feat,
    vals,
    weight,
    bias,
    cot,
    act_out,
    wg_out,
    bg_out,
    win,
    vv,
    wv,
    bv,
    cv,
    actv,
    send1,
    got1,
    mine,
    got2,
    buf_a,
    got_a,
    buf_b,
    got_b,
    buf_c,
    got_c,
    buf_d,
    got_d,
    got_e,
    rows_f,
    full,
    bias_v,
    load_sem,
    hs,
    hr,
    xs,
    xr,
    ps,
    pr,
    rs,
    rr,
    as_,
    ar,
):
    b = lax.axis_index("blk")
    r = lax.axis_index("rep")
    n_blk = 256
    xl = b % 2
    z = (b // 2) % 32
    y = b // 64
    xh = r // 2
    core = r % 2
    x = xh * 2 + xl
    zl = z % ZL
    zh = z // ZL
    up = lax.rem(b + 2, n_blk)
    down = lax.rem(b + n_blk - 2, n_blk)
    across = b + 1 - 2 * xl
    sibling = r + 1 - 2 * core
    far = lax.rem(r + 2, 4)

    def x_dev(q):
        return dev(b - xl + q % 2, (q // 2) * 2 + core)

    def y_dev(w):
        return dev(w * 64 + b % 64, r)

    def zl_dev(j):
        return dev(y * 64 + (zh * ZL + j) * 2 + xl, r)

    def zh_dev(j):
        return dev(y * 64 + (j * ZL + zl) * 2 + xl, r)

    barrier = pltpu.get_barrier_semaphore()
    partners = [dev(up, r), dev(down, r), dev(b, sibling)]
    partners += [x_dev(lax.rem(x + u, X)) for u in range(1, X)]
    partners += [y_dev(lax.rem(y + u, Y)) for u in range(1, Y)]
    partners += [zl_dev(lax.rem(zl + u, ZL)) for u in range(1, ZL)]
    partners += [zh_dev(lax.rem(zh + u, ZH)) for u in range(1, ZH)]
    load_own = pltpu.make_async_copy(
        feat.at[:, pl.ds(pl.multiple_of(r * 32, 32), 32), :], win.at[pl.ds(8 * 8 + 4, 4)], load_sem.at[0]
    )
    load_own.start()
    for to in partners:
        pl.semaphore_signal(barrier, inc=1, device_id=to, device_id_type=pl.DeviceIdType.MESH)
    loads = [
        pltpu.make_async_copy(vals, vv, load_sem.at[1]),
        pltpu.make_async_copy(weight, wv, load_sem.at[2]),
        pltpu.make_async_copy(bias, bv, load_sem.at[3]),
        pltpu.make_async_copy(cot, cv, load_sem.at[4]),
    ]
    for c in loads:
        c.start()
    load_own.wait()
    pl.semaphore_wait(barrier, len(partners))

    def chain(direction, k, chunk):
        off = -k if direction == 0 else k
        to = off - 1 if direction == 0 else off + 1
        first, count = (5, 3) if chunk == 0 else (3, 2)
        return rcopy(
            win.at[pl.ds((off + 8) * 8 + first, count)],
            win.at[pl.ds((to + 8) * 8 + first, count)],
            hs.at[direction, chunk, k],
            hr.at[direction, chunk, k],
            dev(up if direction == 0 else down, r),
        )

    def relay(off, sem):
        return rcopy(
            win.at[pl.ds((off + 8) * 8 + 5, 3)],
            win.at[pl.ds((off + 8) * 8, 3)],
            xs.at[sem],
            xr.at[sem],
            dev(across, r),
        )

    swap = rcopy(win.at[pl.ds(68, 1)], win.at[pl.ds(67, 1)], xs.at[17], xr.at[17], dev(across, r))
    swap.start()
    chain(0, 0, 0).start()
    chain(1, 0, 0).start()
    relay(0, 8).start()
    swap.wait_recv()
    chain(0, 0, 1).start()
    chain(1, 0, 1).start()

    def step(k, _):
        for direction in (0, 1):
            off = -k if direction == 0 else k
            chain(direction, k - 1, 0).wait_recv()
            chain(direction, k, 0).start()
            relay(off, 8 + off).start()
        for direction in (0, 1):
            chain(direction, k - 1, 1).wait_recv()
            chain(direction, k, 1).start()
        return 0

    lax.fori_loop(1, STEPS, step, 0)
    for direction in (0, 1):
        chain(direction, STEPS - 1, 0).wait_recv()
    last = relay(8 - 16 * xl, 0)
    last.start()
    for direction in (0, 1):
        chain(direction, STEPS - 1, 1).wait_recv()
    for c in loads:
        c.wait()

    def relayed(k, _):
        relay(k - 8, k).wait_recv()
        return 0

    lax.fori_loop(1, 16, relayed, 0)
    last.wait_recv()

    def sent(k, _):
        for direction in (0, 1):
            for chunk in (0, 1):
                chain(direction, k, chunk).wait_send()
        return 0

    lax.fori_loop(0, STEPS, sent, 0)

    def relay_sent(k, _):
        relay(k - 8, k).wait_send()
        return 0

    lax.fori_loop(1, 16, relay_sent, 0)
    last.wait_send()
    swap.wait_send()

    slots = 64
    lane_slot = lax.broadcasted_iota(jnp.int32, (8, 32, 128), 0)

    def place(j, s):
        col = cols[j, s]
        e = (col // 4 - b + 16 + n_blk) % n_blk
        t = col % 4
        kk = (e + xl) // 2
        tile = jnp.where(e % 2 == 1, (t + 3) % 4, 4 + t)
        return jnp.minimum(kk * 8 + tile, 135)

    def partial(j):
        count = cnt[j]

        def chunk(c, acc):
            first = c * 8
            picked = jnp.concatenate([win[place(j, first + u)] for u in range(8)], axis=0)
            v = vv[j, pl.ds(first, 8)]
            v = jnp.where(lane_slot + first < count, v, jnp.zeros_like(v)).reshape(256, 128)
            return acc + lax.dot_general(
                v, picked, (((0,), (0,)), ((), ())), preferred_element_type=jnp.float32
            )

        return lax.fori_loop(0, slots // 8, chunk, jnp.zeros((128, 256), jnp.float32))

    to_sibling = []
    for h in (0, 1):
        if STOP > 1:
            send1[h] = partial(h * 2 + 1 - core)
        c = rcopy(send1.at[h], got1.at[h], ps.at[h], pr.at[h], dev(b, sibling))
        c.start()
        to_sibling.append(c)
    for h in (0, 1):
        if STOP > 1:
            mine[h] = partial(h * 2 + core)
    for h in (0, 1):
        to_sibling[h].wait_recv()
    mine[...] = mine[...] + got1[...]
    c = rcopy(mine.at[1 - xh], got2, ps.at[2], pr.at[2], dev(b, far))
    c.start()
    c.wait()
    for h in (0, 1):
        to_sibling[h].wait_send()

    agg = (mine[xh] + got2[...]).astype(jnp.bfloat16)
    pre = jnp.dot(agg, wv[...], preferred_element_type=jnp.float32) + bv[...]
    sig = 1.0 / (1.0 + jnp.exp(-pre))
    actv[...] = (pre * sig).astype(jnp.bfloat16)
    store_act = pltpu.make_async_copy(actv, act_out, load_sem.at[0])
    store_act.start()
    grad = (cv[...].astype(jnp.float32) * sig * (1.0 + pre * (1.0 - sig))).astype(jnp.bfloat16)
    bias_row = jnp.sum(grad.astype(jnp.float32), axis=0, keepdims=True)
    for h in (0, 1):
        buf_a[h, :128] = lax.dot_general(
            agg[:, h * 128 : (h + 1) * 128],
            grad,
            (((0,), (0,)), ((), ())),
            preferred_element_type=jnp.float32,
        )
        buf_a[h, 128:] = jnp.broadcast_to(bias_row, (8, 256))

    pending = []

    def swap_all(n, me, dev_of, src, dst, base):
        copies = []
        for u in range(1, n):
            p = lax.rem(me + u, n)
            c = rcopy(src(p), dst, as_.at[base + u], ar.at[base + u], dev_of(p))
            c.start()
            copies.append(c)
        for c in copies:
            c.wait_recv()
        pending.extend(copies)

    c = rcopy(buf_a.at[1 - core], got_a, as_.at[0], ar.at[0], dev(b, sibling))
    c.start()
    c.wait_recv()
    pending.append(c)
    total = buf_a[core] + got_a[...]
    for q in range(X):
        buf_b[q, :32] = total[q * 32 : (q + 1) * 32]
        buf_b[q, 32:] = total[128:]
    got_b[x] = buf_b[x]
    swap_all(X, x, x_dev, lambda p: buf_b.at[p], got_b.at[x], 0)
    total = got_b[0] + got_b[1] + got_b[2] + got_b[3]
    for w in range(Y):
        buf_c[w, :8] = total[w * 8 : (w + 1) * 8]
        buf_c[w, 8:] = total[32:]
    got_c[y] = buf_c[y]
    swap_all(Y, y, y_dev, lambda p: buf_c.at[p], got_c.at[y], 4)
    total = got_c[0] + got_c[1] + got_c[2] + got_c[3]
    for j in range(ZL):
        buf_d[j, 0:1] = total[j : j + 1]
        buf_d[j, 1:2] = total[8:9]
    got_d[zl] = buf_d[zl]
    swap_all(ZL, zl, zl_dev, lambda p: buf_d.at[p], got_d.at[zl], 8)
    total = got_d[0]
    for j in range(1, ZL):
        total = total + got_d[j]
    got_e[zh] = total
    swap_all(ZH, zh, zh_dev, lambda p: got_e.at[zh], got_e.at[zh], 16)
    total = (got_e[0] + got_e[1] + got_e[2] + got_e[3]) * (1.0 / math.sqrt(131072.0))
    bias_v[...] = total[1:2]
    store_bias = pltpu.make_async_copy(bias_v, bg_out, load_sem.at[1])
    store_bias.start()
    rows_f[zl] = total[0:1]
    swap_all(ZL, zl, zl_dev, lambda p: rows_f.at[zl], rows_f.at[zl], 20)
    at = core * 16 + x * 4 + y
    full[at] = jnp.concatenate([rows_f[j] for j in range(ZL)], axis=0)
    swap_all(Y, y, y_dev, lambda p: full.at[at], full.at[at], 28)
    mid = full.at[pl.ds(core * 16 + x * 4, 4)]
    swap_all(X, x, x_dev, lambda p: mid, mid, 32)
    half = full.at[pl.ds(core * 16, 16)]
    c = rcopy(half, half, as_.at[32], ar.at[32], dev(b, sibling))
    c.start()
    c.wait()
    store_full = pltpu.make_async_copy(full, wg_out, load_sem.at[2])
    store_full.start()
    for c in pending:
        c.wait_send()
    store_act.wait()
    store_bias.wait()
    store_full.wait()


def body(features, tile_vals, tile_cols, tile_count, weight, bias, cotangent):
    f32, bf16 = jnp.float32, jnp.bfloat16
    any_ = pl.BlockSpec(memory_space=pl.ANY)
    smem = pl.BlockSpec(memory_space=pltpu.SMEM)
    act, wg, bg = pl.pallas_call(
        kernel,
        out_shape=[
            jax.ShapeDtypeStruct((128, 256), bf16),
            jax.ShapeDtypeStruct((32, 8, 256), f32),
            jax.ShapeDtypeStruct((1, 256), f32),
        ],
        in_specs=[smem, smem, any_, any_, any_, any_, any_],
        out_specs=[any_, any_, any_],
        scratch_shapes=[
            pltpu.VMEM((17 * 8, 32, 256), bf16),
            pltpu.VMEM((4, 64, 32, 128), bf16),
            pltpu.VMEM((256, 256), bf16),
            pltpu.VMEM((1, 256), f32),
            pltpu.VMEM((128, 256), bf16),
            pltpu.VMEM((128, 256), bf16),
            pltpu.VMEM((2, 128, 256), f32),
            pltpu.VMEM((2, 128, 256), f32),
            pltpu.VMEM((2, 128, 256), f32),
            pltpu.VMEM((128, 256), f32),
            pltpu.VMEM((2, 136, 256), f32),
            pltpu.VMEM((136, 256), f32),
            pltpu.VMEM((4, 40, 256), f32),
            pltpu.VMEM((4, 40, 256), f32),
            pltpu.VMEM((4, 16, 256), f32),
            pltpu.VMEM((4, 16, 256), f32),
            pltpu.VMEM((8, 2, 256), f32),
            pltpu.VMEM((8, 2, 256), f32),
            pltpu.VMEM((4, 2, 256), f32),
            pltpu.VMEM((8, 1, 256), f32),
            pltpu.VMEM((32, 8, 256), f32),
            pltpu.VMEM((1, 256), f32),
            pltpu.SemaphoreType.DMA((5,)),
            pltpu.SemaphoreType.DMA((2, 2, STEPS)),
            pltpu.SemaphoreType.DMA((2, 2, STEPS)),
            pltpu.SemaphoreType.DMA((18,)),
            pltpu.SemaphoreType.DMA((18,)),
            pltpu.SemaphoreType.DMA((3,)),
            pltpu.SemaphoreType.DMA((3,)),
            pltpu.SemaphoreType.DMA((1,)),
            pltpu.SemaphoreType.DMA((1,)),
            pltpu.SemaphoreType.DMA((36,)),
            pltpu.SemaphoreType.DMA((36,)),
        ],
        compiler_params=pltpu.CompilerParams(
            collective_id=0, has_side_effects=True, vmem_limit_bytes=32 * 1024 * 1024
        ),
    )(
        tile_cols,
        tile_count,
        features.reshape(4, 128, 256),
        tile_vals,
        weight,
        bias.reshape(1, 256),
        cotangent,
    )
    return act, wg.reshape(256, 256), bg.reshape(256)


def solution(mesh):
    return jax.shard_map(
        body,
        mesh=mesh,
        in_specs=(
            P("blk", None),
            P("blk", None, "rep", None),
            P("blk", None),
            P("blk"),
            P(),
            P(),
            P(("blk", "rep"), None),
        ),
        out_specs=(P(("blk", "rep"), None), P(), P()),
        check_vma=False,
    )
```

```python
import math

import jax
import jax.numpy as jnp
from jax import lax
from jax.experimental import pallas as pl
from jax.experimental.pallas import tpu as pltpu
from jax.sharding import PartitionSpec as P

STEPS = 8
ZL = 4
ZH = 8
XY = 16
Q = 64
RELAYED = ((Q, 96), (Q + 96, 96))
PLAIN = ((-Q, 2 * Q),)
STOP = 99


def dev(b, r):
    return {"blk": b, "rep": r}


def rcopy(src, dst, ssem, rsem, to):
    return pltpu.make_async_remote_copy(
        src_ref=src,
        dst_ref=dst,
        send_sem=ssem,
        recv_sem=rsem,
        device_id=to,
        device_id_type=pl.DeviceIdType.MESH,
    )


def kernel(
    cols,
    cnt,
    feat,
    vals,
    weight,
    bias,
    cot,
    act_out,
    wg_out,
    bg_out,
    own,
    win,
    vv,
    where_v,
    where_s,
    acc,
    wv,
    bv,
    cv,
    actv,
    got1,
    mine,
    got2,
    buf_a,
    got_a,
    buf_b,
    got_b,
    buf_d,
    got_d,
    got_e,
    rows_f,
    full,
    bias_v,
    load_sem,
    hs,
    hr,
    xs,
    xr,
    ps,
    pr,
    as_,
    ar,
):
    b = lax.axis_index("blk")
    r = lax.axis_index("rep")
    n_blk = 256
    xl = b % 2
    z = (b // 2) % 32
    y = b // 64
    xh = r // 2
    core = r % 2
    x = xh * 2 + xl
    xy = x * 4 + y
    zl = z % ZL
    zh = z // ZL
    up = lax.rem(b + 2, n_blk)
    down = lax.rem(b + n_blk - 2, n_blk)
    across = b + 1 - 2 * xl
    sibling = r + 1 - 2 * core
    far = lax.rem(r + 2, 4)

    def xy_dev(q):
        return dev((q % 4) * 64 + z * 2 + (q // 4) % 2, (q // 8) * 2 + core)

    def zl_dev(j):
        return dev(y * 64 + (zh * ZL + j) * 2 + xl, r)

    def zh_dev(j):
        return dev(y * 64 + (j * ZL + zl) * 2 + xl, r)

    load_own = pltpu.make_async_copy(
        feat.at[:, pl.ds(pl.multiple_of(r * 32, 32), 32), :], own, load_sem.at[0]
    )
    load_own.start()
    barrier = pltpu.get_barrier_semaphore()
    partners = [dev(up, r), dev(down, r), dev(b, sibling)]
    partners += [zl_dev(lax.rem(zl + u, ZL)) for u in range(1, ZL)]
    partners += [zh_dev(lax.rem(zh + u, ZH)) for u in range(1, ZH)]
    partners += [xy_dev(lax.rem(xy + u, XY)) for u in range(1, XY)]
    for to in partners:
        pl.semaphore_signal(barrier, inc=1, device_id=to, device_id_type=pl.DeviceIdType.MESH)
    loads = [
        pltpu.make_async_copy(vals, vv.at[:, pl.ds(0, 64)], load_sem.at[1]),
        pltpu.make_async_copy(weight, wv, load_sem.at[2]),
        pltpu.make_async_copy(bias, bv, load_sem.at[3]),
        pltpu.make_async_copy(cot, cv, load_sem.at[4]),
    ]
    for c in loads:
        c.start()

    load_own.wait()
    win[8, 256:] = own[...].reshape(128, 256).T
    win[16 * (1 - xl), : 256 - Q] = jnp.zeros((256 - Q, 128), jnp.bfloat16)
    for j in range(4):
        vv[j, 64] = jnp.zeros((32, 128), jnp.bfloat16)
    acc[...] = jnp.zeros_like(acc)

    lane = lax.broadcasted_iota(jnp.int32, (1, 256), 1)

    def note_slot(s, found):
        out = []
        for j in range(4):
            col = cols[j, s]
            e = ((col >> 2) - b + 16 + n_blk) & (n_blk - 1)
            at = ((e + xl) >> 1) * 8 + (e & 1) * 4 + (col & 3)
            at = jnp.where(s < cnt[j], at, 1000)
            out.append(jnp.where(lane == at, s, found[j]))
        return tuple(out)

    found = lax.fori_loop(0, 64, note_slot, (jnp.full((1, 256), 64, jnp.int32),) * 4)
    for j in range(4):
        where_v[j : j + 1] = found[j]
    note = pltpu.make_async_copy(where_v, where_s, load_sem.at[5])
    note.start()
    pl.semaphore_wait(barrier, len(partners))

    def chain(direction, k, n):
        off = -k if direction == 0 else k
        to = off - 1 if direction == 0 else off + 1
        first, count = (RELAYED + PLAIN)[n]
        return rcopy(
            win.at[off + 8, pl.ds(256 + first, count)],
            win.at[to + 8, pl.ds(256 + first, count)],
            hs.at[direction, n, k],
            hr.at[direction, n, k],
            dev(up if direction == 0 else down, r),
        )

    def relay(off, n, sem):
        first, count = RELAYED[n]
        return rcopy(
            win.at[off + 8, pl.ds(256 + first, count)],
            win.at[off + 8, pl.ds(first - Q, count)],
            xs.at[n, sem],
            xr.at[n, sem],
            dev(across, r),
        )

    n_rel = len(RELAYED)
    n_all = n_rel + len(PLAIN)
    swap = rcopy(
        win.at[8, pl.ds(256, Q)], win.at[8, pl.ds(256 - Q, Q)], xs.at[0, 17], xr.at[0, 17], dev(across, r)
    )
    swap.start()
    for n in range(n_rel):
        chain(0, 0, n).start()
        chain(1, 0, n).start()
        relay(0, n, 8).start()
    swap.wait_recv()
    for n in range(n_rel, n_all):
        chain(0, 0, n).start()
        chain(1, 0, n).start()
    for c in loads:
        c.wait()
    note.wait()

    def products(places):
        left = []
        for at in places:
            left.append(win[at, 256:])
            left.append(jnp.concatenate([win[at, 256 - Q : 256], win[at, : 256 - Q]], axis=0))
        left = jnp.concatenate(left, axis=1)
        for pair in (0, 1):
            right = []
            for j in (2 * pair, 2 * pair + 1):
                tiles = [vv[j, where_s[j, at * 8 + u]] for at in places for u in range(8)]
                right.append(jnp.concatenate(tiles, axis=0))
            right = jnp.concatenate(right, axis=1)
            out = jnp.dot(left, right, preferred_element_type=jnp.float32)
            acc[2 * pair] += out[:, :128]
            acc[2 * pair + 1] += out[:, 128:]
            if len(places) > 1:
                yield pair

    def relays_in(k):
        for n in range(n_rel):
            relay(-k, n, 8 - k).wait_recv()
            relay(k, n, 8 + k).wait_recv()

    def step(k, _):
        for n in range(n_rel):
            for direction in (0, 1):
                off = -k if direction == 0 else k
                chain(direction, k - 1, n).wait_recv()
                chain(direction, k, n).start()
                relay(off, n, 8 + off).start()
        for n in range(n_rel, n_all):
            for direction in (0, 1):
                chain(direction, k - 1, n).wait_recv()
                chain(direction, k, n).start()

        @pl.when(k > 1)
        def _():
            relays_in(k - 1)
            for _ in products([8 - (k - 1)]):
                pass
            for _ in products([8 + (k - 1)]):
                pass

        return 0

    for n in range(n_rel):
        relay(0, n, 8).wait_recv()
    for _ in products([8]):
        pass
    lax.fori_loop(1, STEPS, step, 0)
    lasts = []
    for n in range(n_rel):
        for direction in (0, 1):
            chain(direction, STEPS - 1, n).wait_recv()
        lasts.append(relay(8 - 16 * xl, n, 0))
        lasts[-1].start()
    relays_in(STEPS - 1)
    for _ in products([1]):
        pass
    for _ in products([15]):
        pass
    for n in range(n_rel, n_all):
        for direction in (0, 1):
            chain(direction, STEPS - 1, n).wait_recv()
    for c in lasts:
        c.wait_recv()
    to_sibling = []
    for pair in products([0, 16]):
        c = rcopy(acc.at[2 * pair + 1 - core], got1.at[pair], ps.at[pair], pr.at[pair], dev(b, sibling))
        c.start()
        to_sibling.append(c)
    other = 1 - xh
    to_sibling[0].wait_recv()
    to_sibling[1].wait_recv()
    mine[...] = acc[2 * other + core] + got1[other]
    c = rcopy(mine, got2, ps.at[2], pr.at[2], dev(b, far))
    c.start()
    kept = acc[2 * xh + core] + got1[xh]

    def sent(k, _):
        for direction in (0, 1):
            for n in range(n_all):
                chain(direction, k, n).wait_send()
        return 0

    lax.fori_loop(0, STEPS, sent, 0)

    def relay_sent(k, _):
        for n in range(n_rel):
            relay(k - 8, n, k).wait_send()
        return 0

    lax.fori_loop(1, 16, relay_sent, 0)
    for d in lasts:
        d.wait_send()
    swap.wait_send()
    for d in to_sibling:
        d.wait_send()
    c.wait()

    agg = (kept + got2[...]).astype(jnp.bfloat16)
    pre = (
        lax.dot_general(
            agg, wv[...], (((0,), (0,)), ((), ())), preferred_element_type=jnp.float32
        )
        + bv[...]
    )
    sig = 1.0 / (1.0 + jnp.exp(-pre))
    grad = (cv[...].astype(jnp.float32) * sig * (1.0 + pre * (1.0 - sig))).astype(jnp.bfloat16)
    bias_row = jnp.sum(grad.astype(jnp.float32), axis=0, keepdims=True)
    for h in (0, 1):
        buf_a[h, :128] = jnp.dot(
            agg[h * 128 : (h + 1) * 128], grad, preferred_element_type=jnp.float32
        )
        buf_a[h, 128:] = jnp.broadcast_to(bias_row, (8, 256))

    pending = []

    def swap_all(n, me, dev_of, src, dst, base):
        copies = []
        for u in range(1, n):
            p = lax.rem(me + u, n)
            c = rcopy(src(p), dst, as_.at[base + u], ar.at[base + u], dev_of(p))
            c.start()
            copies.append(c)
        for c in copies:
            c.wait_recv()
        pending.extend(copies)

    c = rcopy(buf_a.at[1 - core], got_a, as_.at[0], ar.at[0], dev(b, sibling))
    c.start()
    pending.append(c)
    actv[...] = (pre * sig).astype(jnp.bfloat16)
    store_act = pltpu.make_async_copy(actv, act_out, load_sem.at[0])
    store_act.start()
    c.wait_recv()
    total = buf_a[core] + got_a[...]
    for q in range(XY):
        buf_b[q, :8] = total[q * 8 : (q + 1) * 8]
        buf_b[q, 8:] = total[128:]
    got_b[xy] = buf_b[xy]
    swap_all(XY, xy, xy_dev, lambda p: buf_b.at[p], got_b.at[xy], 0)
    total = got_b[0]
    for q in range(1, XY):
        total = total + got_b[q]
    for j in range(ZL):
        buf_d[j, 0:2] = total[2 * j : 2 * j + 2]
        buf_d[j, 2:3] = total[8:9]
    got_d[zl] = buf_d[zl]
    swap_all(ZL, zl, zl_dev, lambda p: buf_d.at[p], got_d.at[zl], 16)
    total = got_d[0]
    for j in range(1, ZL):
        total = total + got_d[j]
    got_e[zh] = total
    swap_all(ZH, zh, zh_dev, lambda p: got_e.at[zh], got_e.at[zh], 20)
    total = got_e[0]
    for j in range(1, ZH):
        total = total + got_e[j]
    total = total * (1.0 / math.sqrt(131072.0))
    rows_f[zl] = total[0:2]
    bias_v[...] = total[2:3]
    store_bias = pltpu.make_async_copy(bias_v, bg_out, load_sem.at[1])
    store_bias.start()
    swap_all(ZL, zl, zl_dev, lambda p: rows_f.at[zl], rows_f.at[zl], 28)
    at = core * XY + xy
    full[at] = jnp.concatenate([rows_f[j] for j in range(ZL)], axis=0)
    swap_all(XY, xy, xy_dev, lambda p: full.at[at], full.at[at], 32)
    half = full.at[pl.ds(core * XY, XY)]
    c = rcopy(half, half, as_.at[32], ar.at[32], dev(b, sibling))
    c.start()
    c.wait()
    store_full = pltpu.make_async_copy(full, wg_out, load_sem.at[2])
    store_full.start()
    for c in pending:
        c.wait_send()
    store_act.wait()
    store_bias.wait()
    store_full.wait()


def hand_over(a, b, c, a_out, b_out, c_out, sem):
    copies = [
        pltpu.make_async_copy(a, a_out, sem.at[0]),
        pltpu.make_async_copy(b, b_out, sem.at[1]),
        pltpu.make_async_copy(c, c_out, sem.at[2]),
    ]
    for d in copies:
        d.start()
    for d in copies:
        d.wait()


def body(features, tile_vals, tile_cols, tile_count, weight, bias, cotangent):
    f32, bf16 = jnp.float32, jnp.bfloat16
    any_ = pl.BlockSpec(memory_space=pl.ANY)
    smem = pl.BlockSpec(memory_space=pltpu.SMEM)
    act, wg, bg = pl.pallas_call(
        kernel,
        out_shape=[
            jax.ShapeDtypeStruct((128, 256), bf16),
            jax.ShapeDtypeStruct((32, 8, 256), f32),
            jax.ShapeDtypeStruct((1, 256), f32),
        ],
        in_specs=[smem, smem, any_, any_, any_, any_, any_],
        out_specs=[any_, any_, any_],
        scratch_shapes=[
            pltpu.VMEM((4, 32, 256), bf16),
            pltpu.VMEM((17, 512, 128), bf16),
            pltpu.VMEM((4, 65, 32, 128), bf16),
            pltpu.VMEM((4, 256), jnp.int32),
            pltpu.SMEM((4, 256), jnp.int32),
            pltpu.VMEM((4, 256, 128), f32),
            pltpu.VMEM((256, 256), bf16),
            pltpu.VMEM((1, 256), f32),
            pltpu.VMEM((128, 256), bf16),
            pltpu.VMEM((128, 256), bf16),
            pltpu.VMEM((2, 256, 128), f32),
            pltpu.VMEM((256, 128), f32),
            pltpu.VMEM((256, 128), f32),
            pltpu.VMEM((2, 136, 256), f32),
            pltpu.VMEM((136, 256), f32),
            pltpu.VMEM((XY, 16, 256), f32),
            pltpu.VMEM((XY, 16, 256), f32),
            pltpu.VMEM((ZL, 3, 256), f32),
            pltpu.VMEM((ZL, 3, 256), f32),
            pltpu.VMEM((ZH, 3, 256), f32),
            pltpu.VMEM((ZL, 2, 256), f32),
            pltpu.VMEM((32, 8, 256), f32),
            pltpu.VMEM((1, 256), f32),
            pltpu.SemaphoreType.DMA((6,)),
            pltpu.SemaphoreType.DMA((2, len(RELAYED + PLAIN), STEPS)),
            pltpu.SemaphoreType.DMA((2, len(RELAYED + PLAIN), STEPS)),
            pltpu.SemaphoreType.DMA((len(RELAYED), 18)),
            pltpu.SemaphoreType.DMA((len(RELAYED), 18)),
            pltpu.SemaphoreType.DMA((3,)),
            pltpu.SemaphoreType.DMA((3,)),
            pltpu.SemaphoreType.DMA((48,)),
            pltpu.SemaphoreType.DMA((48,)),
        ],
        compiler_params=pltpu.CompilerParams(
            collective_id=0, has_side_effects=True, vmem_limit_bytes=62 * 1024 * 1024
        ),
    )(
        tile_cols,
        tile_count,
        features.reshape(4, 128, 256),
        tile_vals,
        weight,
        bias.reshape(1, 256),
        cotangent,
    )
    act, wg, bg = pl.pallas_call(
        hand_over,
        out_shape=[jax.ShapeDtypeStruct(t.shape, t.dtype) for t in (act, wg, bg)],
        in_specs=[any_, any_, any_],
        out_specs=[any_, any_, any_],
        scratch_shapes=[pltpu.SemaphoreType.DMA((3,))],
        compiler_params=pltpu.CompilerParams(vmem_limit_bytes=62 * 1024 * 1024),
    )(act, wg, bg)
    return act, wg.reshape(256, 256), bg.reshape(256)


def solution(mesh):
    return jax.shard_map(
        body,
        mesh=mesh,
        in_specs=(
            P("blk", None),
            P("blk", None, "rep", None),
            P("blk", None),
            P("blk"),
            P(),
            P(),
            P(("blk", "rep"), None),
        ),
        out_specs=(P(("blk", "rep"), None), P(), P()),
        check_vma=False,
    )
```

```python
import math

import jax
import jax.numpy as jnp
from jax import lax
from jax.experimental import pallas as pl
from jax.experimental.pallas import tpu as pltpu
from jax.sharding import PartitionSpec as P

STEPS = 8
ZL = 4
ZH = 8
XY = 16
Q = 64
RELAYED = ((Q, 256 - Q),)
PLAIN = ((-Q, 2 * Q),)
CHUNKS = RELAYED + PLAIN
SKIPS = (0, 2, 4, 6)
STOP = 99


def dev(b, r):
    return {"blk": b, "rep": r}


def rcopy(src, dst, ssem, rsem, to):
    return pltpu.make_async_remote_copy(
        src_ref=src,
        dst_ref=dst,
        send_sem=ssem,
        recv_sem=rsem,
        device_id=to,
        device_id_type=pl.DeviceIdType.MESH,
    )


def kernel(
    cols,
    cnt,
    feat,
    vals,
    weight,
    bias,
    cot,
    act_out,
    wg_out,
    bg_out,
    own,
    win,
    vv,
    where_v,
    where_s,
    acc,
    wv,
    bv,
    cv,
    actv,
    got1,
    mine,
    got2,
    buf_a,
    got_a,
    buf_b,
    got_b,
    buf_d,
    got_d,
    got_e,
    rows_f,
    full,
    bias_v,
    load_sem,
    hs,
    hr,
    xs,
    xr,
    ps,
    pr,
    as_,
    ar,
):
    b = lax.axis_index("blk")
    r = lax.axis_index("rep")
    n_blk = 256
    xl = b % 2
    z = (b // 2) % 32
    y = b // 64
    xh = r // 2
    core = r % 2
    x = xh * 2 + xl
    xy = x * 4 + y
    zl = z % ZL
    zh = z // ZL
    up = lax.rem(b + 2, n_blk)
    down = lax.rem(b + n_blk - 2, n_blk)
    across = b + 1 - 2 * xl
    sibling = r + 1 - 2 * core
    far = lax.rem(r + 2, 4)
    up2 = lax.rem(b + 4, n_blk)
    down2 = lax.rem(b + n_blk - 4, n_blk)

    def xy_dev(q):
        return dev((q % 4) * 64 + z * 2 + (q // 4) % 2, (q // 8) * 2 + core)

    def zl_dev(j):
        return dev(y * 64 + (zh * ZL + j) * 2 + xl, r)

    def zh_dev(j):
        return dev(y * 64 + (j * ZL + zl) * 2 + xl, r)

    load_own = pltpu.make_async_copy(
        feat.at[:, pl.ds(pl.multiple_of(r * 32, 32), 32), :], own, load_sem.at[0]
    )
    load_own.start()
    barrier = pltpu.get_barrier_semaphore()
    partners = [dev(up, r), dev(down, r), dev(b, sibling), dev(up2, r), dev(down2, r)]
    partners += [zl_dev(lax.rem(zl + u, ZL)) for u in range(1, ZL)]
    partners += [zh_dev(lax.rem(zh + u, ZH)) for u in range(1, ZH)]
    partners += [xy_dev(lax.rem(xy + u, XY)) for u in range(1, XY)]
    for to in partners:
        pl.semaphore_signal(barrier, inc=1, device_id=to, device_id_type=pl.DeviceIdType.MESH)
    loads = [
        pltpu.make_async_copy(vals, vv.at[:, pl.ds(0, 64)], load_sem.at[1]),
        pltpu.make_async_copy(weight, wv, load_sem.at[2]),
        pltpu.make_async_copy(bias, bv, load_sem.at[3]),
        pltpu.make_async_copy(cot, cv, load_sem.at[4]),
    ]
    for c in loads:
        c.start()

    load_own.wait()
    win[8, 256:] = own[...].reshape(128, 256).T
    if Q < 256:
        win[16 * (1 - xl), : 256 - Q] = jnp.zeros((256 - Q, 128), jnp.bfloat16)
    pl.semaphore_wait(barrier, len(partners))

    def chain(direction, src, dst, n):
        sign = 2 * direction - 1
        first, count = CHUNKS[n]
        if isinstance(dst, int) and dst - src == 2:
            to = up2 if direction == 0 else down2
        else:
            to = up if direction == 0 else down
        return rcopy(
            win.at[8 + sign * src, pl.ds(256 + first, count)],
            win.at[8 + sign * dst, pl.ds(256 + first, count)],
            hs.at[direction, n, dst - 1],
            hr.at[direction, n, dst - 1],
            dev(to, r),
        )

    def relay(off, n, sem):
        first, count = RELAYED[n]
        return rcopy(
            win.at[off + 8, pl.ds(256 + first, count)],
            win.at[off + 8, pl.ds(first - Q, count)],
            xs.at[n, sem],
            xr.at[n, sem],
            dev(across, r),
        )

    n_rel = len(RELAYED)
    n_all = n_rel + len(PLAIN)
    swap = rcopy(
        win.at[8, pl.ds(256, Q)], win.at[8, pl.ds(256 - Q, Q)], xs.at[0, 17], xr.at[0, 17], dev(across, r)
    )
    swap.start()
    def children(k):
        out = []
        if k in SKIPS and k + 2 <= STEPS:
            out.append(k + 2)
        if k + 1 <= STEPS and k - 1 not in SKIPS:
            out.append(k + 1)
        return out

    for n in range(n_all):
        if CHUNKS[n][0] >= 0:
            for dst in children(0):
                chain(0, 0, dst, n).start()
                chain(1, 0, dst, n).start()
        if n < n_rel:
            relay(0, n, 8).start()
    for j in range(4):
        vv[j, 64] = jnp.zeros((32, 128), jnp.bfloat16)
    acc[...] = jnp.zeros_like(acc)

    lane = lax.broadcasted_iota(jnp.int32, (1, 256), 1)

    def note_slot(s, found):
        out = []
        for j in range(4):
            col = cols[j, s]
            e = ((col >> 2) - b + 16 + n_blk) & (n_blk - 1)
            at = ((e + xl) >> 1) * 8 + (e & 1) * 4 + (col & 3)
            at = jnp.where(s < cnt[j], at, 1000)
            out.append(jnp.where(lane == at, s, found[j]))
        return tuple(out)

    found = lax.fori_loop(0, 64, note_slot, (jnp.full((1, 256), 64, jnp.int32),) * 4)
    for j in range(4):
        where_v[j : j + 1] = found[j]
    note = pltpu.make_async_copy(where_v, where_s, load_sem.at[5])
    note.start()
    swap.wait_recv()
    for n in range(n_all):
        if CHUNKS[n][0] < 0:
            for dst in children(0):
                chain(0, 0, dst, n).start()
                chain(1, 0, dst, n).start()
    for c in loads:
        c.wait()
    note.wait()

    def products(places):
        left = []
        for at in places:
            left.append(win[at, 256:])
            if Q < 256:
                left.append(jnp.concatenate([win[at, 256 - Q : 256], win[at, : 256 - Q]], axis=0))
            else:
                left.append(win[at, :256])
        left = jnp.concatenate(left, axis=1)
        for pair in (1 - xh, xh) if len(places) > 1 else (0, 1):
            right = []
            for j in (2 * pair, 2 * pair + 1):
                tiles = [vv[j, where_s[j, at * 8 + u]] for at in places for u in range(8)]
                right.append(jnp.concatenate(tiles, axis=0))
            right = jnp.concatenate(right, axis=1)
            out = jnp.dot(left, right, preferred_element_type=jnp.float32)
            acc[2 * pair] += out[:, :128]
            acc[2 * pair + 1] += out[:, 128:]
            if len(places) > 1:
                yield pair

    def relays_in(k):
        for n in range(n_rel):
            relay(-k, n, 8 - k).wait_recv()
            relay(k, n, 8 + k).wait_recv()

    def arrivals(k, dsts):
        for n in range(n_all):
            for direction in (0, 1):
                chain(direction, k - 1, k, n).wait_recv()
                for dst in dsts:
                    chain(direction, k, dst, n).start()
                if n < n_rel:
                    off = -k if direction == 0 else k
                    relay(off, n, 8 + off).start()

    def multiply(k):
        relays_in(k)
        for _ in products([8 - k]):
            pass
        for _ in products([8 + k]):
            pass

    for n in range(n_rel):
        relay(0, n, 8).wait_recv()
    for _ in products([8]):
        pass
    tail = max(SKIPS + (-1,)) + 2
    for k in range(1, tail):
        arrivals(k, children(k))
        if k > 1:
            multiply(k - 1)

    def step(k, _):
        arrivals(k, [k + 1])

        @pl.when(k > 1)
        def _():
            multiply(k - 1)

        return 0

    lax.fori_loop(tail, STEPS, step, 0)
    lasts = []
    for n in range(n_rel):
        for direction in (0, 1):
            chain(direction, STEPS - 1, STEPS, n).wait_recv()
        lasts.append(relay(8 - 16 * xl, n, 0))
        lasts[-1].start()
    relays_in(STEPS - 1)
    for _ in products([1]):
        pass
    for _ in products([15]):
        pass
    for n in range(n_rel, n_all):
        for direction in (0, 1):
            chain(direction, STEPS - 1, STEPS, n).wait_recv()
    for c in lasts:
        c.wait_recv()
    to_sibling = []
    for n, pair in enumerate(products([0, 16])):
        c = rcopy(acc.at[2 * pair + 1 - core], got1.at[n], ps.at[n], pr.at[n], dev(b, sibling))
        c.start()
        to_sibling.append(c)
    to_sibling[0].wait_recv()
    mine[...] = acc[2 * (1 - xh) + core] + got1[0]
    c = rcopy(mine, got2, ps.at[2], pr.at[2], dev(b, far))
    c.start()
    to_sibling[1].wait_recv()
    kept = acc[2 * xh + core] + got1[1]

    def sent(k, _):
        for direction in (0, 1):
            for n in range(n_all):
                chain(direction, k - 1, k, n).wait_send()
        return 0

    lax.fori_loop(1, STEPS + 1, sent, 0)

    def relay_sent(k, _):
        for n in range(n_rel):
            relay(k - 8, n, k).wait_send()
        return 0

    lax.fori_loop(1, 16, relay_sent, 0)
    for d in lasts:
        d.wait_send()
    swap.wait_send()
    for d in to_sibling:
        d.wait_send()
    c.wait()

    agg = (kept + got2[...]).astype(jnp.bfloat16)
    pre = (
        lax.dot_general(
            agg, wv[...], (((0,), (0,)), ((), ())), preferred_element_type=jnp.float32
        )
        + bv[...]
    )
    sig = 1.0 / (1.0 + jnp.exp(-pre))
    grad = (cv[...].astype(jnp.float32) * sig * (1.0 + pre * (1.0 - sig))).astype(jnp.bfloat16)
    bias_row = jnp.sum(grad.astype(jnp.float32), axis=0, keepdims=True)
    for h in (0, 1):
        buf_a[h, :128] = jnp.dot(
            agg[h * 128 : (h + 1) * 128], grad, preferred_element_type=jnp.float32
        )
        buf_a[h, 128:] = jnp.broadcast_to(bias_row, (8, 256))

    pending = []

    def swap_all(n, me, dev_of, src, dst, base):
        copies = []
        for u in range(1, n):
            p = lax.rem(me + u, n)
            c = rcopy(src(p), dst, as_.at[base + u], ar.at[base + u], dev_of(p))
            c.start()
            copies.append(c)
        for c in copies:
            c.wait_recv()
        pending.extend(copies)

    c = rcopy(buf_a.at[1 - core], got_a, as_.at[0], ar.at[0], dev(b, sibling))
    c.start()
    pending.append(c)
    actv[...] = (pre * sig).astype(jnp.bfloat16)
    store_act = pltpu.make_async_copy(actv, act_out, load_sem.at[0])
    store_act.start()
    c.wait_recv()
    total = buf_a[core] + got_a[...]
    for q in range(XY):
        buf_b[q, :8] = total[q * 8 : (q + 1) * 8]
        buf_b[q, 8:] = total[128:]
    got_b[xy] = buf_b[xy]
    swap_all(XY, xy, xy_dev, lambda p: buf_b.at[p], got_b.at[xy], 0)
    total = got_b[0]
    for q in range(1, XY):
        total = total + got_b[q]
    for j in range(ZL):
        buf_d[j, 0:2] = total[2 * j : 2 * j + 2]
        buf_d[j, 2:3] = total[8:9]
    got_d[zl] = buf_d[zl]
    swap_all(ZL, zl, zl_dev, lambda p: buf_d.at[p], got_d.at[zl], 16)
    total = got_d[0]
    for j in range(1, ZL):
        total = total + got_d[j]
    got_e[zh] = total
    swap_all(ZH, zh, zh_dev, lambda p: got_e.at[zh], got_e.at[zh], 20)
    total = got_e[0]
    for j in range(1, ZH):
        total = total + got_e[j]
    total = total * (1.0 / math.sqrt(131072.0))
    rows_f[zl] = total[0:2]
    bias_v[...] = total[2:3]
    store_bias = pltpu.make_async_copy(bias_v, bg_out, load_sem.at[1])
    store_bias.start()
    swap_all(ZL, zl, zl_dev, lambda p: rows_f.at[zl], rows_f.at[zl], 28)
    at = core * XY + xy
    full[at] = jnp.concatenate([rows_f[j] for j in range(ZL)], axis=0)
    swap_all(XY, xy, xy_dev, lambda p: full.at[at], full.at[at], 32)
    half = full.at[pl.ds(core * XY, XY)]
    c = rcopy(half, half, as_.at[32], ar.at[32], dev(b, sibling))
    c.start()
    c.wait()
    store_full = pltpu.make_async_copy(full, wg_out, load_sem.at[2])
    store_full.start()
    for c in pending:
        c.wait_send()
    store_act.wait()
    store_bias.wait()
    store_full.wait()


def hand_over(a, b, c, a_out, b_out, c_out):
    a_out[...] = a[...]
    b_out[...] = b[...]
    c_out[...] = c[...]


def body(features, tile_vals, tile_cols, tile_count, weight, bias, cotangent):
    f32, bf16 = jnp.float32, jnp.bfloat16
    any_ = pl.BlockSpec(memory_space=pl.ANY)
    smem = pl.BlockSpec(memory_space=pltpu.SMEM)
    act, wg, bg = pl.pallas_call(
        kernel,
        out_shape=[
            jax.ShapeDtypeStruct((128, 256), bf16),
            jax.ShapeDtypeStruct((32, 8, 256), f32),
            jax.ShapeDtypeStruct((1, 256), f32),
        ],
        in_specs=[smem, smem, any_, any_, any_, any_, any_],
        out_specs=[any_, any_, any_],
        scratch_shapes=[
            pltpu.VMEM((4, 32, 256), bf16),
            pltpu.VMEM((17, 512, 128), bf16),
            pltpu.VMEM((4, 65, 32, 128), bf16),
            pltpu.VMEM((4, 256), jnp.int32),
            pltpu.SMEM((4, 256), jnp.int32),
            pltpu.VMEM((4, 256, 128), f32),
            pltpu.VMEM((256, 256), bf16),
            pltpu.VMEM((1, 256), f32),
            pltpu.VMEM((128, 256), bf16),
            pltpu.VMEM((128, 256), bf16),
            pltpu.VMEM((2, 256, 128), f32),
            pltpu.VMEM((256, 128), f32),
            pltpu.VMEM((256, 128), f32),
            pltpu.VMEM((2, 136, 256), f32),
            pltpu.VMEM((136, 256), f32),
            pltpu.VMEM((XY, 16, 256), f32),
            pltpu.VMEM((XY, 16, 256), f32),
            pltpu.VMEM((ZL, 3, 256), f32),
            pltpu.VMEM((ZL, 3, 256), f32),
            pltpu.VMEM((ZH, 3, 256), f32),
            pltpu.VMEM((ZL, 2, 256), f32),
            pltpu.VMEM((32, 8, 256), f32),
            pltpu.VMEM((1, 256), f32),
            pltpu.SemaphoreType.DMA((6,)),
            pltpu.SemaphoreType.DMA((2, len(CHUNKS), STEPS)),
            pltpu.SemaphoreType.DMA((2, len(CHUNKS), STEPS)),
            pltpu.SemaphoreType.DMA((max(len(RELAYED), 1), 18)),
            pltpu.SemaphoreType.DMA((max(len(RELAYED), 1), 18)),
            pltpu.SemaphoreType.DMA((3,)),
            pltpu.SemaphoreType.DMA((3,)),
            pltpu.SemaphoreType.DMA((48,)),
            pltpu.SemaphoreType.DMA((48,)),
        ],
        compiler_params=pltpu.CompilerParams(
            collective_id=0, has_side_effects=True, vmem_limit_bytes=62 * 1024 * 1024
        ),
    )(
        tile_cols,
        tile_count,
        features.reshape(4, 128, 256),
        tile_vals,
        weight,
        bias.reshape(1, 256),
        cotangent,
    )
    act, wg, bg = pl.pallas_call(
        hand_over,
        out_shape=[jax.ShapeDtypeStruct(t.shape, t.dtype) for t in (act, wg, bg)],
        compiler_params=pltpu.CompilerParams(vmem_limit_bytes=62 * 1024 * 1024),
    )(act, wg, bg)
    return act, wg.reshape(256, 256), bg.reshape(256)


def solution(mesh):
    return jax.shard_map(
        body,
        mesh=mesh,
        in_specs=(
            P("blk", None),
            P("blk", None, "rep", None),
            P("blk", None),
            P("blk"),
            P(),
            P(),
            P(("blk", "rep"), None),
        ),
        out_specs=(P(("blk", "rep"), None), P(), P()),
        check_vma=False,
    )
```

```python
import math

import jax
import jax.numpy as jnp
from jax import lax
from jax.experimental import pallas as pl
from jax.experimental.pallas import tpu as pltpu
from jax.sharding import PartitionSpec as P

STEPS = 8
ZL = 4
ZH = 8
XY = 16
Q = 32
RELAYED = ((Q, 256 - Q),)
PLAIN = ((-Q, 2 * Q),)
CHUNKS = RELAYED + PLAIN
SKIPS = (0, 2, 4, 6)


def dev(b, r):
    return {"blk": b, "rep": r}


def rcopy(src, dst, ssem, rsem, to):
    return pltpu.make_async_remote_copy(
        src_ref=src,
        dst_ref=dst,
        send_sem=ssem,
        recv_sem=rsem,
        device_id=to,
        device_id_type=pl.DeviceIdType.MESH,
    )


def kernel(
    cols,
    cnt,
    feat,
    vals,
    weight,
    bias,
    cot,
    act_out,
    wg_out,
    bg_out,
    own,
    win,
    vv,
    where_v,
    where_s,
    acc,
    wv,
    bv,
    cv,
    actv,
    got1,
    mine,
    got2,
    buf_a,
    got_a,
    buf_b,
    got_b,
    buf_d,
    got_d,
    got_e,
    rows_f,
    full,
    bias_v,
    load_sem,
    hs,
    hr,
    xs,
    xr,
    ps,
    pr,
    as_,
    ar,
):
    b = lax.axis_index("blk")
    r = lax.axis_index("rep")
    n_blk = 256
    xl = b % 2
    z = (b // 2) % 32
    y = b // 64
    xh = r // 2
    core = r % 2
    x = xh * 2 + xl
    xy = x * 4 + y
    zl = z % ZL
    zh = z // ZL
    up = lax.rem(b + 2, n_blk)
    down = lax.rem(b + n_blk - 2, n_blk)
    across = b + 1 - 2 * xl
    sibling = r + 1 - 2 * core
    far = lax.rem(r + 2, 4)
    up2 = lax.rem(b + 4, n_blk)
    down2 = lax.rem(b + n_blk - 4, n_blk)

    def xy_dev(q):
        return dev((q % 4) * 64 + z * 2 + (q // 4) % 2, (q // 8) * 2 + core)

    def zl_dev(j):
        return dev(y * 64 + (zh * ZL + j) * 2 + xl, r)

    def zh_dev(j):
        return dev(y * 64 + (j * ZL + zl) * 2 + xl, r)

    load_own = pltpu.make_async_copy(
        feat.at[:, pl.ds(pl.multiple_of(r * 32, 32), 32), :], own, load_sem.at[0]
    )
    load_own.start()
    barrier = pltpu.get_barrier_semaphore()
    partners = [dev(up, r), dev(down, r), dev(b, sibling), dev(up2, r), dev(down2, r)]
    partners += [zl_dev(lax.rem(zl + u, ZL)) for u in range(1, ZL)]
    partners += [zh_dev(lax.rem(zh + u, ZH)) for u in range(1, ZH)]
    partners += [xy_dev(lax.rem(xy + u, XY)) for u in range(1, XY)]
    for to in partners:
        pl.semaphore_signal(barrier, inc=1, device_id=to, device_id_type=pl.DeviceIdType.MESH)
    loads = [
        pltpu.make_async_copy(vals, vv.at[:, pl.ds(0, 64)], load_sem.at[1]),
        pltpu.make_async_copy(weight, wv, load_sem.at[2]),
        pltpu.make_async_copy(bias, bv, load_sem.at[3]),
        pltpu.make_async_copy(cot, cv, load_sem.at[4]),
    ]
    for c in loads:
        c.start()

    load_own.wait()
    win[8, 256:] = own[...].reshape(128, 256).T
    if Q < 256:
        win[16 * (1 - xl), : 256 - Q] = jnp.zeros((256 - Q, 128), jnp.bfloat16)
    pl.semaphore_wait(barrier, len(partners))

    def chain(direction, src, dst, n):
        sign = 2 * direction - 1
        first, count = CHUNKS[n]
        if isinstance(dst, int) and dst - src == 2:
            to = up2 if direction == 0 else down2
        else:
            to = up if direction == 0 else down
        return rcopy(
            win.at[8 + sign * src, pl.ds(256 + first, count)],
            win.at[8 + sign * dst, pl.ds(256 + first, count)],
            hs.at[direction, n, dst - 1],
            hr.at[direction, n, dst - 1],
            dev(to, r),
        )

    def relay(off, n, sem):
        first, count = RELAYED[n]
        return rcopy(
            win.at[off + 8, pl.ds(256 + first, count)],
            win.at[off + 8, pl.ds(first - Q, count)],
            xs.at[n, sem],
            xr.at[n, sem],
            dev(across, r),
        )

    n_rel = len(RELAYED)
    n_all = n_rel + len(PLAIN)
    swap = rcopy(
        win.at[8, pl.ds(256, Q)], win.at[8, pl.ds(256 - Q, Q)], xs.at[0, 17], xr.at[0, 17], dev(across, r)
    )
    swap.start()
    def children(k):
        out = []
        if k in SKIPS and k + 2 <= STEPS:
            out.append(k + 2)
        if k + 1 <= STEPS and k - 1 not in SKIPS:
            out.append(k + 1)
        return out

    for n in range(n_all):
        if CHUNKS[n][0] >= 0:
            for dst in children(0):
                chain(0, 0, dst, n).start()
                chain(1, 0, dst, n).start()
        if n < n_rel:
            relay(0, n, 8).start()
    for j in range(4):
        vv[j, 64] = jnp.zeros((32, 128), jnp.bfloat16)
    acc[...] = jnp.zeros_like(acc)

    lane = lax.broadcasted_iota(jnp.int32, (1, 256), 1)

    def note_slot(s, found):
        out = []
        for j in range(4):
            col = cols[j, s]
            e = ((col >> 2) - b + 16 + n_blk) & (n_blk - 1)
            at = ((e + xl) >> 1) * 8 + (e & 1) * 4 + (col & 3)
            at = jnp.where(s < cnt[j], at, 1000)
            out.append(jnp.where(lane == at, s, found[j]))
        return tuple(out)

    found = lax.fori_loop(0, 64, note_slot, (jnp.full((1, 256), 64, jnp.int32),) * 4)
    for j in range(4):
        where_v[j : j + 1] = found[j]
    note = pltpu.make_async_copy(where_v, where_s, load_sem.at[5])
    note.start()
    swap.wait_recv()
    for n in range(n_all):
        if CHUNKS[n][0] < 0:
            for dst in children(0):
                chain(0, 0, dst, n).start()
                chain(1, 0, dst, n).start()
    for c in loads:
        c.wait()
    note.wait()

    def products(places):
        left = []
        for at in places:
            left.append(win[at, 256:])
            if Q < 256:
                left.append(jnp.concatenate([win[at, 256 - Q : 256], win[at, : 256 - Q]], axis=0))
            else:
                left.append(win[at, :256])
        left = jnp.concatenate(left, axis=1)
        for pair in (1 - xh, xh) if len(places) > 1 else (0, 1):
            right = []
            for j in (2 * pair, 2 * pair + 1):
                tiles = [vv[j, where_s[j, at * 8 + u]] for at in places for u in range(8)]
                right.append(jnp.concatenate(tiles, axis=0))
            right = jnp.concatenate(right, axis=1)
            out = jnp.dot(left, right, preferred_element_type=jnp.float32)
            acc[2 * pair] += out[:, :128]
            acc[2 * pair + 1] += out[:, 128:]
            if len(places) > 1:
                yield pair

    def relays_in(k):
        for n in range(n_rel):
            relay(-k, n, 8 - k).wait_recv()
            relay(k, n, 8 + k).wait_recv()

    def arrivals(k, dsts):
        for n in range(n_all):
            for direction in (0, 1):
                chain(direction, k - 1, k, n).wait_recv()
                for dst in dsts:
                    chain(direction, k, dst, n).start()
                if n < n_rel:
                    off = -k if direction == 0 else k
                    relay(off, n, 8 + off).start()

    def multiply(k):
        relays_in(k)
        for _ in products([8 - k]):
            pass
        for _ in products([8 + k]):
            pass

    for n in range(n_rel):
        relay(0, n, 8).wait_recv()
    for _ in products([8]):
        pass
    tail = max(SKIPS + (-1,)) + 2
    for k in range(1, tail):
        arrivals(k, children(k))
        if k > 1:
            multiply(k - 1)

    def step(k, _):
        arrivals(k, [k + 1])

        @pl.when(k > 1)
        def _():
            multiply(k - 1)

        return 0

    lax.fori_loop(tail, STEPS, step, 0)
    lasts = []
    for n in range(n_rel):
        for direction in (0, 1):
            chain(direction, STEPS - 1, STEPS, n).wait_recv()
        lasts.append(relay(8 - 16 * xl, n, 0))
        lasts[-1].start()
    relays_in(STEPS - 1)
    for _ in products([1]):
        pass
    for _ in products([15]):
        pass
    for n in range(n_rel, n_all):
        for direction in (0, 1):
            chain(direction, STEPS - 1, STEPS, n).wait_recv()
    for c in lasts:
        c.wait_recv()
    to_sibling = []
    for n, pair in enumerate(products([0, 16])):
        c = rcopy(acc.at[2 * pair + 1 - core], got1.at[n], ps.at[n], pr.at[n], dev(b, sibling))
        c.start()
        to_sibling.append(c)
    to_sibling[0].wait_recv()
    mine[...] = acc[2 * (1 - xh) + core] + got1[0]
    c = rcopy(mine, got2, ps.at[2], pr.at[2], dev(b, far))
    c.start()
    to_sibling[1].wait_recv()
    kept = acc[2 * xh + core] + got1[1]

    def sent(k, _):
        for direction in (0, 1):
            for n in range(n_all):
                chain(direction, k - 1, k, n).wait_send()
        return 0

    lax.fori_loop(1, STEPS + 1, sent, 0)

    def relay_sent(k, _):
        for n in range(n_rel):
            relay(k - 8, n, k).wait_send()
        return 0

    lax.fori_loop(1, 16, relay_sent, 0)
    for d in lasts:
        d.wait_send()
    swap.wait_send()
    for d in to_sibling:
        d.wait_send()
    c.wait()

    agg = (kept + got2[...]).astype(jnp.bfloat16)
    pre = (
        lax.dot_general(
            agg, wv[...], (((0,), (0,)), ((), ())), preferred_element_type=jnp.float32
        )
        + bv[...]
    )
    sig = 1.0 / (1.0 + jnp.exp(-pre))
    grad = (cv[...].astype(jnp.float32) * sig * (1.0 + pre * (1.0 - sig))).astype(jnp.bfloat16)
    bias_row = jnp.sum(grad.astype(jnp.float32), axis=0, keepdims=True)
    for h in (0, 1):
        buf_a[h, :128] = jnp.dot(
            agg[h * 128 : (h + 1) * 128], grad, preferred_element_type=jnp.float32
        )
        buf_a[h, 128:] = jnp.broadcast_to(bias_row, (8, 256))

    pending = []

    def swap_all(n, me, dev_of, src, dst, base):
        copies = []
        for u in range(1, n):
            p = lax.rem(me + u, n)
            c = rcopy(src(p), dst, as_.at[base + u], ar.at[base + u], dev_of(p))
            c.start()
            copies.append(c)
        for c in pending:
            c.wait_send()
        pending.clear()
        for c in copies:
            c.wait_recv()
        pending.extend(copies)

    c = rcopy(buf_a.at[1 - core], got_a, as_.at[0], ar.at[0], dev(b, sibling))
    c.start()
    pending.append(c)
    actv[...] = (pre * sig).astype(jnp.bfloat16)
    store_act = pltpu.make_async_copy(actv, act_out, load_sem.at[0])
    store_act.start()
    c.wait_recv()
    total = buf_a[core] + got_a[...]
    for q in range(XY):
        buf_b[q, :8] = total[q * 8 : (q + 1) * 8]
        buf_b[q, 8:] = total[128:]
    got_b[xy] = buf_b[xy]
    swap_all(XY, xy, xy_dev, lambda p: buf_b.at[p], got_b.at[xy], 0)
    total = got_b[0]
    for q in range(1, XY):
        total = total + got_b[q]
    for j in range(ZL):
        buf_d[j, 0:2] = total[2 * j : 2 * j + 2]
        buf_d[j, 2:3] = total[8:9]
    got_d[zl] = buf_d[zl]
    swap_all(ZL, zl, zl_dev, lambda p: buf_d.at[p], got_d.at[zl], 16)
    total = got_d[0]
    for j in range(1, ZL):
        total = total + got_d[j]
    got_e[zh] = total
    swap_all(ZH, zh, zh_dev, lambda p: got_e.at[zh], got_e.at[zh], 20)
    total = got_e[0]
    for j in range(1, ZH):
        total = total + got_e[j]
    total = total * (1.0 / math.sqrt(131072.0))
    rows_f[zl] = total[0:2]
    bias_v[...] = total[2:3]
    store_bias = pltpu.make_async_copy(bias_v, bg_out, load_sem.at[1])
    store_bias.start()
    swap_all(ZL, zl, zl_dev, lambda p: rows_f.at[zl], rows_f.at[zl], 28)
    at = core * XY + xy
    full[at] = jnp.concatenate([rows_f[j] for j in range(ZL)], axis=0)
    swap_all(XY, xy, xy_dev, lambda p: full.at[at], full.at[at], 32)
    half = full.at[pl.ds(core * XY, XY)]
    c = rcopy(half, half, as_.at[32], ar.at[32], dev(b, sibling))
    c.start()
    for d in pending:
        d.wait_send()
    c.wait()
    store_full = pltpu.make_async_copy(full, wg_out, load_sem.at[2])
    store_full.start()
    store_act.wait()
    store_bias.wait()
    store_full.wait()


def hand_over(a, b, c, a_out, b_out, c_out):
    a_out[...] = a[...]
    b_out[...] = b[...]
    c_out[...] = c[...]


def body(features, tile_vals, tile_cols, tile_count, weight, bias, cotangent):
    f32, bf16 = jnp.float32, jnp.bfloat16
    any_ = pl.BlockSpec(memory_space=pl.ANY)
    smem = pl.BlockSpec(memory_space=pltpu.SMEM)
    act, wg, bg = pl.pallas_call(
        kernel,
        out_shape=[
            jax.ShapeDtypeStruct((128, 256), bf16),
            jax.ShapeDtypeStruct((32, 8, 256), f32),
            jax.ShapeDtypeStruct((1, 256), f32),
        ],
        in_specs=[smem, smem, any_, any_, any_, any_, any_],
        out_specs=[any_, any_, any_],
        scratch_shapes=[
            pltpu.VMEM((4, 32, 256), bf16),
            pltpu.VMEM((17, 512, 128), bf16),
            pltpu.VMEM((4, 65, 32, 128), bf16),
            pltpu.VMEM((4, 256), jnp.int32),
            pltpu.SMEM((4, 256), jnp.int32),
            pltpu.VMEM((4, 256, 128), f32),
            pltpu.VMEM((256, 256), bf16),
            pltpu.VMEM((1, 256), f32),
            pltpu.VMEM((128, 256), bf16),
            pltpu.VMEM((128, 256), bf16),
            pltpu.VMEM((2, 256, 128), f32),
            pltpu.VMEM((256, 128), f32),
            pltpu.VMEM((256, 128), f32),
            pltpu.VMEM((2, 136, 256), f32),
            pltpu.VMEM((136, 256), f32),
            pltpu.VMEM((XY, 16, 256), f32),
            pltpu.VMEM((XY, 16, 256), f32),
            pltpu.VMEM((ZL, 3, 256), f32),
            pltpu.VMEM((ZL, 3, 256), f32),
            pltpu.VMEM((ZH, 3, 256), f32),
            pltpu.VMEM((ZL, 2, 256), f32),
            pltpu.VMEM((32, 8, 256), f32),
            pltpu.VMEM((1, 256), f32),
            pltpu.SemaphoreType.DMA((6,)),
            pltpu.SemaphoreType.DMA((2, len(CHUNKS), STEPS)),
            pltpu.SemaphoreType.DMA((2, len(CHUNKS), STEPS)),
            pltpu.SemaphoreType.DMA((max(len(RELAYED), 1), 18)),
            pltpu.SemaphoreType.DMA((max(len(RELAYED), 1), 18)),
            pltpu.SemaphoreType.DMA((3,)),
            pltpu.SemaphoreType.DMA((3,)),
            pltpu.SemaphoreType.DMA((48,)),
            pltpu.SemaphoreType.DMA((48,)),
        ],
        compiler_params=pltpu.CompilerParams(
            collective_id=0, has_side_effects=True, vmem_limit_bytes=62 * 1024 * 1024
        ),
    )(
        tile_cols,
        tile_count,
        features.reshape(4, 128, 256),
        tile_vals,
        weight,
        bias.reshape(1, 256),
        cotangent,
    )
    act, wg, bg = pl.pallas_call(
        hand_over,
        out_shape=[jax.ShapeDtypeStruct(t.shape, t.dtype) for t in (act, wg, bg)],
        compiler_params=pltpu.CompilerParams(vmem_limit_bytes=62 * 1024 * 1024),
    )(act, wg, bg)
    return act, wg.reshape(256, 256), bg.reshape(256)


def solution(mesh):
    return jax.shard_map(
        body,
        mesh=mesh,
        in_specs=(
            P("blk", None),
            P("blk", None, "rep", None),
            P("blk", None),
            P("blk"),
            P(),
            P(),
            P(("blk", "rep"), None),
        ),
        out_specs=(P(("blk", "rep"), None), P(), P()),
        check_vma=False,
    )
```
